256 devices in a mesh: bin: 4 (over z_lo, core), frame: 64 (over y, z_hi, x).
Axes of the slice: x: 4, y: 4, z: 8 (z_hi: 4, z_lo: 2; z = z_hi * 2 + z_lo), core: 2. Of those that a mesh axis runs over, the one named last changes fastest.
Arguments:
- signal: bfloat16 [32, 2, 256, 16384], P('bin', None, None, 'frame'), may hold values from -24 to 24
- demix: float32 [32, 256, 512], P('bin'), may hold values from -1 to 2
Outputs:
- demixed: float32 [32, 256, 512], P('bin', 'frame')
- gradient: float32 [32, 256, 512], P('bin', 'frame')
The draws below stay inside these ranges and needn't reach their ends.
All inputs are finite; a program needn't handle non-finite values.
Results may differ from the reference program's by a relative error of at most 0.0061.
Values sent between devices are 32-bit elements; how exact they have to be, the bound alone decides.
No kernel may reach another device: no remote copies, remote signals or barrier semaphores. Data moves between devices by JAX's collectives and lax.ppermute only.
A program may use at most 64 MiB of HBM per device.

```python
import math
import jax
import jax.numpy as jnp
from jax import lax

SENSOR_COUNT = 256
BINS = 32
ITERS = 2
TIME_FRAMES = 16384


def draw_signal(key, part):
    root_key, frequency_key, channel_key, pulse_key, frame_key = jax.random.split(jax.random.fold_in(key, 11), 5)
    shape = (BINS, 2, SENSOR_COUNT, TIME_FRAMES)
    root_seed = jnp.clip(jax.random.normal(root_key, shape, jnp.float32), -4.0, 4.0)
    frame_lo, frame_hi = (0.5, 2.0)
    bin_channel = jnp.exp(jax.random.uniform(frequency_key, (BINS, 1, SENSOR_COUNT, 1), jnp.float32, 0.0, math.log(3.0)))
    channel_scale = jnp.exp(jax.random.uniform(channel_key, (1, 1, SENSOR_COUNT, 1), jnp.float32, 0.0, math.log(2.0)))
    pulse_event = jnp.exp(jax.random.uniform(pulse_key, (1, 1, SENSOR_COUNT, TIME_FRAMES), jnp.float32, math.log(0.5), math.log(2.0)))
    frame_factor = jnp.exp(jax.random.uniform(frame_key, (1, 1, 1, TIME_FRAMES), jnp.float32, math.log(frame_lo), math.log(frame_hi)))
    return (0.25 * root_seed * bin_channel * channel_scale * pulse_event * frame_factor).astype(jnp.bfloat16)


def draw_demix(key, part):
    root_key = jax.random.fold_in(key, 23)
    shape = (BINS, SENSOR_COUNT, 2 * SENSOR_COUNT)
    root_seed = jnp.clip(jax.random.normal(root_key, shape, jnp.float32), -4.0, 4.0)
    row_ids = jnp.arange(SENSOR_COUNT).reshape(1, SENSOR_COUNT, 1)
    col_ids = jnp.arange(2 * SENSOR_COUNT).reshape(1, 1, 2 * SENSOR_COUNT)
    identity = jnp.where(row_ids == col_ids, 1.0, 0.0).astype(jnp.float32)
    return identity + 0.5 * root_seed / math.sqrt(SENSOR_COUNT)


def setup_inputs(seed: int = 0) -> dict:
    seeds = jax.random.split(jax.random.key(seed), 3)
    signal = draw_signal(jax.random.fold_in(seeds[2], 71), 0)
    demix = draw_demix(jax.random.fold_in(seeds[2], 71), 0)
    return dict(signal=signal, demix=demix)


step_size = 0.05
small_eps = 1e-06

def complex_matrix(demixing):
    width = demixing.shape[-1] // 2
    real_part = demixing[..., :width]
    imag_part = demixing[..., width:]
    upper = jnp.concatenate([real_part, imag_part], axis=-1)
    lower = jnp.concatenate([-imag_part, real_part], axis=-1)
    return jnp.concatenate([upper, lower], axis=-2)

def stack_signal(spectra):
    real_part = spectra[:, 0]
    imag_part = spectra[:, 1]
    upper = jnp.concatenate([real_part, imag_part], axis=-1)
    lower = jnp.concatenate([-imag_part, real_part], axis=-1)
    return jnp.concatenate([upper, lower], axis=-2)

def reference(signal, demix):
    frame_total = signal.shape[-1]
    demixing = demix
    direction = jnp.zeros_like(demix)
    for iteration in range(ITERS):
        rounded = demixing.astype(jnp.bfloat16)

        def one_bin(pair):
            weights, spectra = pair
            stacked = stack_signal(spectra[None])[0]
            return jnp.dot(weights, stacked, preferred_element_type=jnp.float32)
        sources = lax.map(one_bin, (rounded, signal))
        squares = lax.optimization_barrier(jnp.sum(sources * sources, axis=0))
        power_sum = squares[:, :frame_total] + squares[:, frame_total:]
        radius = jnp.sqrt(power_sum / BINS + small_eps)
        radius_both = jnp.concatenate([radius, radius], axis=1)

        def one_gram(values):
            scored = (values / radius_both).astype(jnp.bfloat16)
            source_b = values.astype(jnp.bfloat16)
            imag_key = jnp.concatenate([-source_b[:, frame_total:], source_b[:, :frame_total]], axis=1)
            dims = (((1,), (1,)), ((), ()))
            real_gram = lax.dot_general(scored, source_b, dims, preferred_element_type=jnp.float32)
            imag_gram = lax.dot_general(scored, imag_key, dims, preferred_element_type=jnp.float32)
            return jnp.concatenate([real_gram, imag_gram], axis=1) / frame_total
        gram_full = lax.map(one_gram, sources)
        product = jnp.einsum('fkj,fjl->fkl', gram_full, complex_matrix(demixing), precision=lax.Precision.HIGHEST)
        direction = demixing - product
        demixing = demixing + step_size * direction
    return (demixing, direction)
```

```python
import jax
import jax.numpy as jnp
import numpy as np
from jax import lax
from jax.experimental import pallas as pl
from jax.experimental.pallas import tpu as pltpu
from jax.sharding import PartitionSpec as P

BINS = 32
ITERS = 2

step_size = 0.05
small_eps = 1e-06

X1, X3, Y1, Y3, Z1, Z3 = 1, 3, 16, 48, 4, 12
CHAINS = (
    (0, 4, (X1, X3, Y1, Y3, Z1, Z3), (Y1, Y3, X1, X3, Z1, Z3)),
    (4, 4, (X3, X1, Y3, Y1, Z3, Z1), (Y3, Y1, X3, X1, Z3, Z1)),
)
STEPS = 6
GROUP = 64


def owner_table(masks):
    table = np.zeros(GROUP, np.int32)
    for place in range(GROUP):
        for step in range(STEPS):
            if place >> (STEPS - 1 - step) & 1:
                table[place] ^= masks[step]
    return table


def exchange(value, chain, step):
    pairs = []
    for b in range(4):
        mask = chain[2 + b % 2][step]
        pairs += [(b * GROUP + f, b * GROUP + (f ^ mask)) for f in range(GROUP)]
    return lax.ppermute(value, ("bin", "frame"), pairs)


def over_bins(value, mask):
    return lax.ppermute(value, "bin", [(b, b ^ mask) for b in range(4)])


def nt_dot(a, b):
    return lax.dot_general(a, b, (((1,), (1,)), ((), ())), preferred_element_type=jnp.float32)


def nn_dot(a, b):
    return lax.dot_general(a, b, (((1,), (0,)), ((), ())), preferred_element_type=jnp.float32)


def tn_dot(a, b):
    return lax.dot_general(a, b, (((0,), (0,)), ((), ())), preferred_element_type=jnp.float32)


def sources_body(core_ref, wb, x_ref, y_ref, mine_ref, other_ref, power):
    step = pl.program_id(0)
    frames = x_ref.shape[-1]
    real_x = x_ref[0, 0]
    imag_x = x_ref[0, 1]
    real_y = nn_dot(wb, jnp.concatenate([real_x, -imag_x], axis=0))
    imag_y = nn_dot(wb, jnp.concatenate([imag_x, real_x], axis=0))
    y_ref[0, :, :frames] = real_y
    y_ref[0, :, frames:] = imag_y
    squares = real_y * real_y + imag_y * imag_y

    @pl.when(step == 0)
    def _():
        power[...] = squares

    @pl.when(step > 0)
    def _():
        power[...] += squares

    @pl.when(step == pl.num_programs(0) - 1)
    def _():
        half = power.shape[0] // 2
        core = core_ref[0]
        mine_ref[...] = power[pl.ds(pl.multiple_of(core * half, half), half), :]
        other_ref[...] = power[pl.ds(pl.multiple_of((1 - core) * half, half), half), :]


def first_sources_kernel(core_ref, w_ref, x_ref, y_ref, mine_ref, other_ref, power):
    wb = w_ref[0].astype(jnp.bfloat16)
    sources_body(core_ref, wb, x_ref, y_ref, mine_ref, other_ref, power)


def next_sources_kernel(core_ref, *refs):
    pieces = refs[: 2 * len(CHAINS)]
    place_ref, x_ref, y_ref, mine_ref, other_ref, power, wb_ref = refs[2 * len(CHAINS) :]
    step = pl.program_id(0)
    half = pieces[0].shape[1]
    for c, chain in enumerate(CHAINS):

        @pl.when(jnp.logical_and(step >= chain[0], step < chain[0] + chain[1]))
        def _(c=c):
            low = pieces[2 * c][0].astype(jnp.bfloat16)
            high = pieces[2 * c + 1][0].astype(jnp.bfloat16)
            moved = tn_dot(place_ref[c], jnp.concatenate([low, high], axis=0))
            wb_ref[...] = moved.astype(jnp.bfloat16)

    sources_body(core_ref, wb_ref[...], x_ref, y_ref, mine_ref, other_ref, power)


def sources_outputs(bins, rows, frames):
    half = rows // 2
    whole = lambda f, *_: (0, 0)
    return dict(
        out_specs=[
            pl.BlockSpec((1, rows, 2 * frames), lambda f, *_: (f, 0, 0)),
            pl.BlockSpec((half, frames), whole),
            pl.BlockSpec((half, frames), whole),
        ],
        shapes=[
            jax.ShapeDtypeStruct((bins, rows, 2 * frames), jnp.float32),
            jax.ShapeDtypeStruct((half, frames), jnp.float32),
            jax.ShapeDtypeStruct((half, frames), jnp.float32),
        ],
    )


def first_sources(core, demix, signal):
    bins, rows, width = demix.shape
    frames = signal.shape[-1]
    outs = sources_outputs(bins, rows, frames)
    return pl.pallas_call(
        first_sources_kernel,
        grid_spec=pltpu.PrefetchScalarGridSpec(
            num_scalar_prefetch=1,
            grid=(bins,),
            in_specs=[
                pl.BlockSpec((1, rows, width), lambda f, *_: (f, 0, 0)),
                pl.BlockSpec((1, 2, rows, frames), lambda f, *_: (f, 0, 0, 0)),
            ],
            out_specs=outs["out_specs"],
            scratch_shapes=[pltpu.VMEM((rows, frames), jnp.float32)],
        ),
        out_shape=outs["shapes"],
        cost_estimate=pl.CostEstimate(
            flops=2 * bins * rows * width * 2 * frames, bytes_accessed=bins * rows * 10 * frames, transcendentals=0
        ),
        name="first_sources",
    )(core, demix, signal)


def next_sources(core, pieces, place, signal):
    bins, _, rows, frames = signal.shape
    width = pieces[0].shape[-1]
    outs = sources_outputs(bins, rows, frames)
    specs = []
    for start, count, _, _ in CHAINS:
        spec = pl.BlockSpec(
            (1, rows // 2, width),
            lambda f, *_, start=start, count=count: (jnp.clip(f - start, 0, count - 1), 0, 0),
        )
        specs += [spec, spec]
    specs.append(pl.BlockSpec(place.shape, lambda f, *_: (0, 0, 0)))
    specs.append(pl.BlockSpec((1, 2, rows, frames), lambda f, *_: (f, 0, 0, 0)))
    return pl.pallas_call(
        next_sources_kernel,
        grid_spec=pltpu.PrefetchScalarGridSpec(
            num_scalar_prefetch=1,
            grid=(bins,),
            in_specs=specs,
            out_specs=outs["out_specs"],
            scratch_shapes=[
                pltpu.VMEM((rows, frames), jnp.float32),
                pltpu.VMEM((rows, width), jnp.bfloat16),
            ],
        ),
        out_shape=outs["shapes"],
        cost_estimate=pl.CostEstimate(
            flops=3 * bins * rows * width * 2 * frames, bytes_accessed=bins * rows * 10 * frames, transcendentals=0
        ),
        name="next_sources",
    )(core, *pieces, place, signal)


def gram_kernel(core_ref, y_ref, mine_ref, other_ref, place_ref, keep_ref, send_ref, inverse):
    frames = mine_ref.shape[1]

    @pl.when(pl.program_id(0) == 0)
    def _():
        half = mine_ref.shape[0]
        core = core_ref[0]
        for ref, at in ((mine_ref, core), (other_ref, 1 - core)):
            radius = jnp.sqrt(ref[...] / BINS + small_eps)
            inverse[pl.ds(pl.multiple_of(at * half, half), half), :] = 1.0 / radius

    real_y = y_ref[0, :, :frames]
    imag_y = y_ref[0, :, frames:]
    scale = inverse[...]
    scored = jnp.concatenate(
        [(real_y * scale).astype(jnp.bfloat16), (imag_y * scale).astype(jnp.bfloat16)], axis=1
    )
    scored = nn_dot(place_ref[...], scored).astype(jnp.bfloat16)
    real_b = real_y.astype(jnp.bfloat16)
    imag_b = imag_y.astype(jnp.bfloat16)
    real_g = nt_dot(scored, jnp.concatenate([real_b, imag_b], axis=1))
    imag_g = nt_dot(scored, jnp.concatenate([-imag_b, real_b], axis=1))
    rows = real_g.shape[0]
    half = rows // 2
    keep_ref[0, :, :rows] = real_g[:half]
    keep_ref[0, :, rows:] = imag_g[:half]
    send_ref[0, :, :rows] = real_g[half:]
    send_ref[0, :, rows:] = imag_g[half:]


def gram(core, y, mine, other, place, chain):
    _, rows, both = y.shape
    frames = both // 2
    first, count = chain[0], chain[1]
    half = rows // 2
    whole = lambda f, *_: (0, 0)
    out_spec = pl.BlockSpec((1, half, 2 * rows), lambda f, *_: (f, 0, 0))
    out_shape = jax.ShapeDtypeStruct((count, half, 2 * rows), jnp.float32)
    return pl.pallas_call(
        gram_kernel,
        grid_spec=pltpu.PrefetchScalarGridSpec(
            num_scalar_prefetch=1,
            grid=(count,),
            in_specs=[
                pl.BlockSpec((1, rows, both), lambda f, *_: (f + first, 0, 0)),
                pl.BlockSpec((half, frames), whole),
                pl.BlockSpec((half, frames), whole),
                pl.BlockSpec((rows, rows), whole),
            ],
            out_specs=[out_spec, out_spec],
            scratch_shapes=[pltpu.VMEM((rows, frames), jnp.float32)],
        ),
        out_shape=[out_shape, out_shape],
        cost_estimate=pl.CostEstimate(
            flops=3 * count * rows * both * 2 * rows, bytes_accessed=count * rows * 8 * both, transcendentals=rows * frames
        ),
        name="gram",
    )(core, y, mine, other, place)


def reduce_rows(keep, send, chain):
    for step in range(STEPS):
        total = keep + exchange(send, chain, step)
        if step + 1 == STEPS:
            return total
        half = total.shape[1] // 2
        keep = total[:, :half]
        send = total[:, half:]


def gather_rows(rows, chain):
    for step in reversed(range(STEPS)):
        received = exchange(rows, chain, step)
        if step == 0:
            return rows, received
        rows = jnp.concatenate([rows, received], axis=1)


def exact(spec, a, b):
    return jnp.einsum(spec, a, b, precision=lax.Precision.HIGHEST, preferred_element_type=jnp.float32)


def direction(own, gram_rows, pieces, place, frame_total):
    count, r, both = gram_rows.shape
    n = both // 2
    stacked = jnp.concatenate([gram_rows[:, :, :n], gram_rows[:, :, n:]], axis=1) / frame_total
    if place is not None:
        stacked = exact("fsl,pl->fsp", stacked, place.astype(jnp.float32))
    product = 0.0
    at = 0
    for piece in pieces:
        product += exact("fsj,fjl->fsl", stacked[:, :, at : at + piece.shape[1]], piece)
        at += piece.shape[1]
    real_part = product[:, :r, :n] - product[:, r:, n:]
    imag_part = product[:, :r, n:] + product[:, r:, :n]
    return own - jnp.concatenate([real_part, imag_part], axis=-1)


def on_device(signal, demix):
    frame_total = signal.shape[-1] * lax.axis_size("frame")
    rows = demix.shape[1]
    me = lax.axis_index("frame")
    core = lax.axis_index("bin") % 2
    core_in = jnp.reshape(core, (1,)).astype(jnp.int32)
    r = rows // GROUP
    places = []
    for chain in CHAINS:
        table = jnp.where(core == 0, owner_table(chain[2]), owner_table(chain[3]))
        source = ((table ^ me) * r)[:, None] + jnp.arange(r)[None, :]
        places.append((source.reshape(rows, 1) == jnp.arange(rows)[None, :]).astype(jnp.bfloat16))
    place_all = jnp.stack(places)

    own = [lax.dynamic_slice_in_dim(demix[c[0] : c[0] + c[1]], me * r, r, 1) for c in CHAINS]
    pieces = [(demix[c[0] : c[0] + c[1]],) for c in CHAINS]
    directions = own
    for iteration in range(ITERS):
        if iteration == 0:
            y, mine, other = first_sources(core_in, demix, signal)
        else:
            y, mine, other = next_sources(core_in, [p for pair in pieces for p in pair], place_all, signal)
        mine = mine + over_bins(other, 1)
        mine = mine + over_bins(mine, 2)
        other = over_bins(mine, 1)
        parts = [gram(core_in, y, mine, other, p, c) for p, c in zip(places, CHAINS)]
        sums = [reduce_rows(keep, send, c) for (keep, send), c in zip(parts, CHAINS)]
        directions = [
            direction(o, g, p, None if iteration == 0 else place, frame_total)
            for o, g, p, place in zip(own, sums, pieces, places)
        ]
        own = [o + step_size * d for o, d in zip(own, directions)]
        if iteration + 1 < ITERS:
            pieces = [gather_rows(o, c) for o, c in zip(own, CHAINS)]
    return jnp.concatenate(own, axis=0), jnp.concatenate(directions, axis=0)


def solution(mesh):
    placed = (P("bin", None, None, "frame"), P("bin", None, None))
    return jax.shard_map(
        on_device,
        mesh=mesh,
        in_specs=placed,
        out_specs=(P("bin", "frame", None), P("bin", "frame", None)),
        check_vma=False,
    )
```

```python
import functools

import jax
import jax.numpy as jnp
from jax import lax
from jax.experimental import pallas as pl
from jax.experimental.pallas import tpu as pltpu
from jax.sharding import PartitionSpec as P

BINS = 32
ITERS = 2

step_size = 0.05
small_eps = 1e-06

X1, X3, Y1, Y3, Z1, Z3 = 1, 3, 16, 48, 4, 12
CHAINS = (
    (0, 4, (X1, X3, Y1, Y3, Z1, Z3), (Y1, Y3, X1, X3, Z1, Z3)),
    (4, 4, (X3, X1, Y3, Y1, Z3, Z1), (Y3, Y1, X3, X1, Z3, Z1)),
)
STEPS = 6
GROUP = 64


def place_matrix(index_ref, chain, rows):
    core, me = index_ref[0], index_ref[1]
    r = rows // GROUP
    p = lax.broadcasted_iota(jnp.int32, (rows, 1), 0)
    owner = jnp.zeros((rows, 1), jnp.int32) + me
    for step in range(STEPS):
        mask = jnp.where(core == 0, chain[2][step], chain[3][step])
        bit = (p // (r << (STEPS - 1 - step))) & 1
        owner = owner ^ (bit * mask)
    source = owner * r + (p & (r - 1))
    column = lax.broadcasted_iota(jnp.int32, (rows, rows), 1)
    return jnp.where(source == column, 1.0, 0.0).astype(jnp.bfloat16)


def move(value, mask0, mask1):
    pairs = []
    for b in range(4):
        mask = (mask0, mask1)[b % 2]
        pairs += [(b * GROUP + f, b * GROUP + (f ^ mask)) for f in range(GROUP)]
    return lax.ppermute(value, ("bin", "frame"), pairs)


def exchange(value, chain, step):
    return move(value, chain[2][step], chain[3][step])


def over_bins(value, mask):
    return lax.ppermute(value, "bin", [(b, b ^ mask) for b in range(4)])


def nt_dot(a, b):
    return lax.dot_general(a, b, (((1,), (1,)), ((), ())), preferred_element_type=jnp.float32)


def nn_dot(a, b):
    return lax.dot_general(a, b, (((1,), (0,)), ((), ())), preferred_element_type=jnp.float32)


def tn_dot(a, b):
    return lax.dot_general(a, b, (((0,), (0,)), ((), ())), preferred_element_type=jnp.float32)


VMEM_LIMIT = 32 * 2**20
FIRST_LIMIT = 45 * 2**20


def in_vmem(count):
    return [pl.BlockSpec(memory_space=pltpu.VMEM)] * count


def add_sources(f, wb, real_x, imag_x, y_ref, power):
    frames = real_x.shape[-1]
    real_y = nn_dot(wb, jnp.concatenate([real_x, -imag_x], axis=0))
    imag_y = nn_dot(wb, jnp.concatenate([imag_x, real_x], axis=0))
    y_ref[f, :, :frames] = real_y
    y_ref[f, :, frames:] = imag_y
    squares = real_y * real_y + imag_y * imag_y
    power[...] = squares if f == 0 else power[...] + squares


def share_power(core_ref, mine_ref, other_ref, power):
    half = power.shape[0] // 2
    core = core_ref[0]
    mine_ref[...] = power[pl.ds(pl.multiple_of(core * half, half), half), :]
    other_ref[...] = power[pl.ds(pl.multiple_of((1 - core) * half, half), half), :]


def first_sources_kernel(core_ref, w_hbm, x_ref, y_ref, mine_ref, other_ref, place_ref, w_ref, power, w_sem):
    bins = w_ref.shape[0]
    copies = [pltpu.make_async_copy(w_hbm.at[f], w_ref.at[f], w_sem.at[f]) for f in range(bins)]
    for copy in copies:
        copy.start()
    for c, chain in enumerate(CHAINS):
        place_ref[c] = place_matrix(core_ref, chain, w_ref.shape[1])
    for f in range(bins):
        copies[f].wait()
        add_sources(f, w_ref[f].astype(jnp.bfloat16), x_ref[f, 0], x_ref[f, 1], y_ref, power)
    share_power(core_ref, mine_ref, other_ref, power)


def next_sources_kernel(core_ref, *refs):
    pieces = refs[: 2 * len(CHAINS)]
    place_ref, x_ref, y_ref, mine_ref, other_ref, power = refs[2 * len(CHAINS) :]
    for c, chain in enumerate(CHAINS):
        for i in range(chain[1]):
            f = chain[0] + i
            low = pieces[2 * c][i].astype(jnp.bfloat16)
            high = pieces[2 * c + 1][i].astype(jnp.bfloat16)
            wb = tn_dot(place_ref[c], jnp.concatenate([low, high], axis=0)).astype(jnp.bfloat16)
            add_sources(f, wb, x_ref[f, 0], x_ref[f, 1], y_ref, power)
    share_power(core_ref, mine_ref, other_ref, power)


def sources_shapes(bins, rows, frames):
    half = jax.ShapeDtypeStruct((rows // 2, frames), jnp.float32)
    return [jax.ShapeDtypeStruct((bins, rows, 2 * frames), jnp.float32), half, half]


def first_sources(core, demix, signal):
    bins, rows, width = demix.shape
    frames = signal.shape[-1]
    return pl.pallas_call(
        first_sources_kernel,
        in_specs=[pl.BlockSpec(memory_space=pltpu.SMEM), pl.BlockSpec(memory_space=pl.ANY)] + in_vmem(1),
        out_specs=in_vmem(4),
        out_shape=sources_shapes(bins, rows, frames)
        + [jax.ShapeDtypeStruct((len(CHAINS), rows, rows), jnp.bfloat16)],
        scratch_shapes=[
            pltpu.VMEM(demix.shape, demix.dtype),
            pltpu.VMEM((rows, frames), jnp.float32),
            pltpu.SemaphoreType.DMA((bins,)),
        ],
        cost_estimate=pl.CostEstimate(
            flops=2 * bins * rows * width * 2 * frames, bytes_accessed=8 * bins * rows * width, transcendentals=0
        ),
        compiler_params=pltpu.CompilerParams(vmem_limit_bytes=FIRST_LIMIT),
        name="first_sources",
    )(core, demix, signal)


def next_sources(core, pieces, place, signal):
    bins, _, rows, frames = signal.shape
    return pl.pallas_call(
        next_sources_kernel,
        in_specs=[pl.BlockSpec(memory_space=pltpu.SMEM)] + in_vmem(len(pieces) + 2),
        out_specs=in_vmem(3),
        out_shape=sources_shapes(bins, rows, frames),
        scratch_shapes=[pltpu.VMEM((rows, frames), jnp.float32)],
        cost_estimate=pl.CostEstimate(
            flops=3 * bins * rows * 2 * rows * 2 * frames, bytes_accessed=8 * bins * rows * 2 * frames, transcendentals=0
        ),
        compiler_params=pltpu.CompilerParams(vmem_limit_bytes=VMEM_LIMIT),
        name="next_sources",
    )(core, *pieces, place, signal)


def gram_kernel(c, core_ref, y_ref, mine_ref, other_ref, place_ref, keep_ref, send_ref, inverse):
    half, frames = mine_ref.shape
    first = CHAINS[c][0]
    core = core_ref[0]
    for ref, at in ((mine_ref, core), (other_ref, 1 - core)):
        radius = jnp.sqrt(ref[...] / BINS + small_eps)
        inverse[pl.ds(pl.multiple_of(at * half, half), half), :] = 1.0 / radius
    for i in range(keep_ref.shape[0]):
        real_y = y_ref[first + i, :, :frames]
        imag_y = y_ref[first + i, :, frames:]
        scale = inverse[...]
        scored = jnp.concatenate(
            [(real_y * scale).astype(jnp.bfloat16), (imag_y * scale).astype(jnp.bfloat16)], axis=1
        )
        scored = nn_dot(place_ref[c], scored).astype(jnp.bfloat16)
        real_b = real_y.astype(jnp.bfloat16)
        imag_b = imag_y.astype(jnp.bfloat16)
        real_g = nt_dot(scored, jnp.concatenate([real_b, imag_b], axis=1))
        imag_g = nt_dot(scored, jnp.concatenate([-imag_b, real_b], axis=1))
        rows = 2 * half
        send_ref[i, :, :rows] = real_g[half:]
        send_ref[i, :, rows:] = imag_g[half:]
        keep_ref[i, :, :rows] = real_g[:half]
        keep_ref[i, :, rows:] = imag_g[:half]


def gram(core, y, mine, other, place, c):
    _, rows, both = y.shape
    count = CHAINS[c][1]
    out_shape = jax.ShapeDtypeStruct((count, rows // 2, 2 * rows), jnp.float32)
    return pl.pallas_call(
        functools.partial(gram_kernel, c),
        in_specs=[pl.BlockSpec(memory_space=pltpu.SMEM)] + in_vmem(4),
        out_specs=in_vmem(2),
        out_shape=[out_shape, out_shape],
        scratch_shapes=[pltpu.VMEM((rows, both // 2), jnp.float32)],
        cost_estimate=pl.CostEstimate(
            flops=3 * count * rows * both * 2 * rows, bytes_accessed=count * rows * 4 * both, transcendentals=rows * both
        ),
        compiler_params=pltpu.CompilerParams(vmem_limit_bytes=VMEM_LIMIT),
        name="gram",
    )(core, y, mine, other, place)


def reduce_rows(keep, send, chain):
    for step in range(STEPS):
        received = exchange(send, chain, step)
        if step + 1 == STEPS:
            return keep, received
        half = keep.shape[1] // 2
        send = keep[:, half:] + received[:, half:]
        keep = keep[:, :half] + received[:, :half]


def gather_rows(own):
    first, second = CHAINS[0][2][4:]
    from_z = {0: own}
    for mask in (first, second, first ^ second):
        from_z[mask] = move(own, mask, mask)
    pieces = []
    for chain in CHAINS:
        first, second = chain[2][4:]
        span = slice(chain[0], chain[0] + chain[1])
        order = (0, second, first, first ^ second)
        rows = lax.optimization_barrier(jnp.concatenate([from_z[m][span] for m in order], axis=1))
        for step in reversed(range(STEPS - 2)):
            received = exchange(rows, chain, step)
            if step > 0:
                rows = lax.optimization_barrier(jnp.concatenate([rows, received], axis=1))
        pieces.append((rows, received))
    return pieces


def split(value):
    high = value.astype(jnp.bfloat16)
    rest = value - high.astype(jnp.float32)
    middle = rest.astype(jnp.bfloat16)
    low = (rest - middle.astype(jnp.float32)).astype(jnp.bfloat16)
    return high, middle, low


def exact_dot(a, b):
    rows = a.shape[0]
    parts = split(a)
    total = 0.0
    for i, part in enumerate(split(b)):
        sums = nn_dot(jnp.concatenate(parts[: 3 - i], axis=0), part)
        for j in range(3 - i):
            total += sums[rows * j : rows * (j + 1)]
    return total


def reorder(value, place):
    rows = value.shape[0]
    sums = nt_dot(jnp.concatenate(split(value), axis=0), place)
    return sums[:rows] + sums[rows : 2 * rows] + sums[2 * rows :]


def direction_kernel(frame_total, ordered, *refs):
    chains = len(CHAINS)
    sums = refs[: 2 * chains]
    own_ref = refs[2 * chains]
    weights = refs[2 * chains + 1 : -2]
    new_ref, direction_ref = refs[-2:]
    r = own_ref.shape[1]
    n = own_ref.shape[2] // 2
    for c, (first, count, _, _) in enumerate(CHAINS):
        stacked = []
        for i in range(count):
            g = (sums[2 * c][i] + sums[2 * c + 1][i]) * (1.0 / frame_total)
            stacked.append(jnp.concatenate([g[:, :n], g[:, n:]], axis=0))
        if not ordered:
            moved = reorder(jnp.concatenate(stacked, axis=0), weights[-1][c])
            stacked = [moved[2 * r * i : 2 * r * (i + 1)] for i in range(count)]
        for i in range(count):
            f = first + i
            if ordered:
                product = exact_dot(stacked[i], weights[0][f])
            else:
                half = n // 2
                product = exact_dot(stacked[i][:, :half], weights[2 * c][i]) + exact_dot(
                    stacked[i][:, half:], weights[2 * c + 1][i]
                )
            real_part = product[:r, :n] - product[r:, n:]
            imag_part = product[:r, n:] + product[r:, :n]
            own = own_ref[f]
            result = own - jnp.concatenate([real_part, imag_part], axis=1)
            direction_ref[f] = result
            new_ref[f] = own + step_size * result


def direction(sums, own, weights, frame_total, ordered):
    shape = jax.ShapeDtypeStruct(own.shape, jnp.float32)
    bins, r, width = own.shape
    return pl.pallas_call(
        functools.partial(direction_kernel, frame_total, ordered),
        in_specs=in_vmem(len(sums) + 1 + len(weights)),
        out_specs=in_vmem(2),
        out_shape=[shape, shape],
        cost_estimate=pl.CostEstimate(
            flops=24 * bins * width * width * 2 * r, bytes_accessed=2 * bins * width * width, transcendentals=0
        ),
        compiler_params=pltpu.CompilerParams(vmem_limit_bytes=VMEM_LIMIT),
        name="direction",
    )(*sums, own, *weights)


def on_device(signal, demix):
    frame_total = signal.shape[-1] * lax.axis_size("frame")
    r = demix.shape[1] // GROUP
    me = lax.axis_index("frame")
    index = jnp.stack([lax.axis_index("bin") % 2, me]).astype(jnp.int32)
    own = lax.dynamic_slice_in_dim(demix, me * r, r, 1)
    index, own, demix, signal = lax.optimization_barrier((index, own, demix, signal))
    weights = [demix]
    for iteration in range(ITERS):
        if iteration == 0:
            y, mine, other, place = first_sources(index, demix, signal)
        else:
            y, mine, other = next_sources(index, weights, place, signal)
        mine = mine + over_bins(other, 1)
        mine = mine + over_bins(mine, 2)
        other = over_bins(mine, 1)
        parts = [gram(index, y, mine, other, place, c) for c in range(len(CHAINS))]
        sums = [s for (keep, send), c in zip(parts, CHAINS) for s in reduce_rows(keep, send, c)]
        own, result = direction(
            sums, own, weights + [place] * iteration, frame_total, iteration == 0
        )
        if iteration + 1 < ITERS:
            weights = [p for pair in gather_rows(own) for p in pair]
    return own, result


def solution(mesh):
    placed = (P("bin", None, None, "frame"), P("bin", None, None))
    return jax.shard_map(
        on_device,
        mesh=mesh,
        in_specs=placed,
        out_specs=(P("bin", "frame", None), P("bin", "frame", None)),
        check_vma=False,
    )
```

```python
import functools

import jax
import jax.numpy as jnp
from jax import lax
from jax.experimental import pallas as pl
from jax.experimental.pallas import tpu as pltpu
from jax.sharding import PartitionSpec as P

BINS = 32
ITERS = 2

step_size = 0.05
small_eps = 1e-06

X1, X3, Y1, Y3, Z1, Z3 = 1, 3, 16, 48, 4, 12
ORDER_A = ((X1, X3, Y1, Y3, Z1, Z3), (Y1, Y3, X1, X3, Z1, Z3))
ORDER_B = ((X3, X1, Y3, Y1, Z3, Z1), (Y3, Y1, X3, X1, Z3, Z1))
CHAINS = ((0, 2, *ORDER_A), (2, 2, *ORDER_A), (4, 2, *ORDER_B), (6, 2, *ORDER_B))
PAIR = 2
LARGE_STEPS = 2
STEPS = 6
GROUP = 64


def place_matrix(index_ref, chain, rows):
    core, me = index_ref[0], index_ref[1]
    r = rows // GROUP
    p = lax.broadcasted_iota(jnp.int32, (rows, 1), 0)
    owner = jnp.zeros((rows, 1), jnp.int32) + me
    for step in range(STEPS):
        mask = jnp.where(core == 0, chain[2][step], chain[3][step])
        bit = (p // (r << (STEPS - 1 - step))) & 1
        owner = owner ^ (bit * mask)
    source = owner * r + (p & (r - 1))
    column = lax.broadcasted_iota(jnp.int32, (rows, rows), 1)
    return jnp.where(source == column, 1.0, 0.0).astype(jnp.bfloat16)


def move(value, mask0, mask1):
    pairs = []
    for b in range(4):
        mask = (mask0, mask1)[b % 2]
        pairs += [(b * GROUP + f, b * GROUP + (f ^ mask)) for f in range(GROUP)]
    return lax.ppermute(value, ("bin", "frame"), pairs)


def exchange(value, chain, step):
    return move(value, chain[2][step], chain[3][step])


def over_bins(value, mask):
    return lax.ppermute(value, "bin", [(b, b ^ mask) for b in range(4)])


def nt_dot(a, b):
    return lax.dot_general(a, b, (((1,), (1,)), ((), ())), preferred_element_type=jnp.float32)


def nn_dot(a, b):
    return lax.dot_general(a, b, (((1,), (0,)), ((), ())), preferred_element_type=jnp.float32)


def tn_dot(a, b):
    return lax.dot_general(a, b, (((0,), (0,)), ((), ())), preferred_element_type=jnp.float32)


VMEM_LIMIT = 32 * 2**20
FIRST_LIMIT = 45 * 2**20


def in_vmem(count):
    return [pl.BlockSpec(memory_space=pltpu.VMEM)] * count


def add_sources(f, wb, real_x, imag_x, y_ref, power):
    frames = real_x.shape[-1]
    real_y = nn_dot(wb, jnp.concatenate([real_x, -imag_x], axis=0))
    imag_y = nn_dot(wb, jnp.concatenate([imag_x, real_x], axis=0))
    y_ref[f, :, :frames] = real_y
    y_ref[f, :, frames:] = imag_y
    squares = real_y * real_y + imag_y * imag_y
    power[...] = squares if f == 0 else power[...] + squares


def share_power(core_ref, mine_ref, other_ref, power):
    half = power.shape[0] // 2
    core = core_ref[0]
    mine_ref[...] = power[pl.ds(pl.multiple_of(core * half, half), half), :]
    other_ref[...] = power[pl.ds(pl.multiple_of((1 - core) * half, half), half), :]


def first_sources_kernel(core_ref, w_hbm, x_ref, y_ref, mine_ref, other_ref, place_ref, own_ref, w_ref, power, w_sem):
    bins, r = own_ref.shape[:2]
    me = core_ref[1]
    copies = [pltpu.make_async_copy(w_hbm.at[f], w_ref.at[f], w_sem.at[f]) for f in range(bins)]
    for copy in copies:
        copy.start()
    for c, chain in enumerate(CHAINS[::PAIR]):
        place_ref[c] = place_matrix(core_ref, chain, w_ref.shape[1])
    for f in range(bins):
        copies[f].wait()
        add_sources(f, w_ref[f].astype(jnp.bfloat16), x_ref[f, 0], x_ref[f, 1], y_ref, power)
        value = w_ref[f, pl.ds(pl.multiple_of((me // 2) * (2 * r), 2 * r), 2 * r), :]
        own_ref[f] = jnp.where(me % 2 == 0, value[:r], value[r:])
    share_power(core_ref, mine_ref, other_ref, power)


def next_sources_kernel(core_ref, *refs):
    pieces = refs[: 2 * len(CHAINS)]
    place_ref, x_ref, y_ref, mine_ref, other_ref, power = refs[2 * len(CHAINS) :]
    for c, chain in enumerate(CHAINS):
        for i in range(chain[1]):
            f = chain[0] + i
            low = pieces[2 * c][i].astype(jnp.bfloat16)
            high = pieces[2 * c + 1][i].astype(jnp.bfloat16)
            wb = tn_dot(place_ref[c // PAIR], jnp.concatenate([low, high], axis=0)).astype(jnp.bfloat16)
            add_sources(f, wb, x_ref[f, 0], x_ref[f, 1], y_ref, power)
    share_power(core_ref, mine_ref, other_ref, power)


def sources_shapes(bins, rows, frames):
    half = jax.ShapeDtypeStruct((rows // 2, frames), jnp.float32)
    return [jax.ShapeDtypeStruct((bins, rows, 2 * frames), jnp.float32), half, half]


def first_sources(core, demix, signal):
    bins, rows, width = demix.shape
    frames = signal.shape[-1]
    return pl.pallas_call(
        first_sources_kernel,
        in_specs=[pl.BlockSpec(memory_space=pltpu.SMEM), pl.BlockSpec(memory_space=pl.ANY)] + in_vmem(1),
        out_specs=in_vmem(5),
        out_shape=sources_shapes(bins, rows, frames)
        + [jax.ShapeDtypeStruct((len(CHAINS) // PAIR, rows, rows), jnp.bfloat16)]
        + [jax.ShapeDtypeStruct((bins, rows // GROUP, width), jnp.float32)],
        scratch_shapes=[
            pltpu.VMEM(demix.shape, demix.dtype),
            pltpu.VMEM((rows, frames), jnp.float32),
            pltpu.SemaphoreType.DMA((bins,)),
        ],
        cost_estimate=pl.CostEstimate(
            flops=2 * bins * rows * width * 2 * frames, bytes_accessed=8 * bins * rows * width, transcendentals=0
        ),
        compiler_params=pltpu.CompilerParams(vmem_limit_bytes=FIRST_LIMIT),
        name="first_sources",
    )(core, demix, signal)


def next_sources(core, pieces, place, signal):
    bins, _, rows, frames = signal.shape
    return pl.pallas_call(
        next_sources_kernel,
        in_specs=[pl.BlockSpec(memory_space=pltpu.SMEM)] + in_vmem(len(pieces) + 2),
        out_specs=in_vmem(3),
        out_shape=sources_shapes(bins, rows, frames),
        scratch_shapes=[pltpu.VMEM((rows, frames), jnp.float32)],
        cost_estimate=pl.CostEstimate(
            flops=3 * bins * rows * 2 * rows * 2 * frames, bytes_accessed=8 * bins * rows * 2 * frames, transcendentals=0
        ),
        compiler_params=pltpu.CompilerParams(vmem_limit_bytes=VMEM_LIMIT),
        name="next_sources",
    )(core, *pieces, place, signal)


def gram_kernel(c, core_ref, y_ref, mine_ref, other_ref, place_ref, keep_ref, send_ref, inverse):
    half, frames = mine_ref.shape
    first = CHAINS[c][0]
    core = core_ref[0]
    for ref, at in ((mine_ref, core), (other_ref, 1 - core)):
        inverse[pl.ds(pl.multiple_of(at * half, half), half), :] = lax.rsqrt(ref[...] / BINS + small_eps)
    for i in range(keep_ref.shape[0]):
        real_y = y_ref[first + i, :, :frames]
        imag_y = y_ref[first + i, :, frames:]
        scale = inverse[...]
        scored = jnp.concatenate(
            [(real_y * scale).astype(jnp.bfloat16), (imag_y * scale).astype(jnp.bfloat16)], axis=1
        )
        scored = nn_dot(place_ref[c // PAIR], scored).astype(jnp.bfloat16)
        real_b = real_y.astype(jnp.bfloat16)
        imag_b = imag_y.astype(jnp.bfloat16)
        real_g = nt_dot(scored, jnp.concatenate([real_b, imag_b], axis=1))
        imag_g = nt_dot(scored, jnp.concatenate([-imag_b, real_b], axis=1))
        rows = 2 * half
        send_ref[i, :, :rows] = real_g[half:]
        send_ref[i, :, rows:] = imag_g[half:]
        keep_ref[i, :, :rows] = real_g[:half]
        keep_ref[i, :, rows:] = imag_g[:half]


def gram(core, y, mine, other, place, c):
    _, rows, both = y.shape
    count = CHAINS[c][1]
    out_shape = jax.ShapeDtypeStruct((count, rows // 2, 2 * rows), jnp.float32)
    return pl.pallas_call(
        functools.partial(gram_kernel, c),
        in_specs=[pl.BlockSpec(memory_space=pltpu.SMEM)] + in_vmem(4),
        out_specs=in_vmem(2),
        out_shape=[out_shape, out_shape],
        scratch_shapes=[pltpu.VMEM((rows, both // 2), jnp.float32)],
        cost_estimate=pl.CostEstimate(
            flops=3 * count * rows * both * 2 * rows, bytes_accessed=count * rows * 4 * both, transcendentals=rows * both
        ),
        compiler_params=pltpu.CompilerParams(vmem_limit_bytes=VMEM_LIMIT),
        name="gram",
    )(core, y, mine, other, place)


def reduce_rows(parts):
    ends = []
    for p in range(0, len(CHAINS), PAIR):
        halves = []
        for (keep, send), chain in zip(parts[p : p + PAIR], CHAINS[p : p + PAIR]):
            for step in range(LARGE_STEPS):
                received = exchange(send, chain, step)
                half = keep.shape[1] // 2
                send = keep[:, half:] + received[:, half:]
                keep = keep[:, :half] + received[:, :half]
            halves.append((keep, send))
        keep, send = (jnp.concatenate(both, axis=0) for both in zip(*halves))
        for step in range(LARGE_STEPS, STEPS):
            received = exchange(send, CHAINS[p], step)
            if step + 1 < STEPS:
                half = keep.shape[1] // 2
                send = keep[:, half:] + received[:, half:]
                keep = keep[:, :half] + received[:, :half]
        ends += [keep, received]
    return ends


def joined(first, second):
    return lax.optimization_barrier(jnp.concatenate([first, second], axis=1))


def gather_rows(own):
    first, second = CHAINS[0][2][4:]
    from_z = {0: own}
    for mask in (first, second, first ^ second):
        from_z[mask] = move(own, mask, mask)
    pieces = []
    for p in range(0, len(CHAINS), PAIR):
        chain = CHAINS[p]
        first, second = chain[2][4:]
        span = slice(chain[0], chain[0] + PAIR * chain[1])
        order = (0, second, first, first ^ second)
        rows = lax.optimization_barrier(jnp.concatenate([from_z[m][span] for m in order], axis=1))
        for step in reversed(range(LARGE_STEPS + 1, STEPS - 2)):
            rows = joined(rows, exchange(rows, chain, step))
        received = exchange(rows, chain, LARGE_STEPS)
        for c in range(PAIR):
            bins = slice(c * chain[1], (c + 1) * chain[1])
            piece = joined(rows[bins], received[bins])
            for step in reversed(range(1, LARGE_STEPS)):
                piece = joined(piece, exchange(piece, chain, step))
            pieces += [piece, exchange(piece, chain, 0)]
    return pieces


def split(value):
    high = value.astype(jnp.bfloat16)
    rest = value - high.astype(jnp.float32)
    middle = rest.astype(jnp.bfloat16)
    low = (rest - middle.astype(jnp.float32)).astype(jnp.bfloat16)
    return high, middle, low


def exact_dot(a, b):
    rows = a.shape[0]
    parts = split(a)
    total = 0.0
    for i, part in enumerate(split(b)):
        sums = nn_dot(jnp.concatenate(parts[: 3 - i], axis=0), part)
        for j in range(3 - i):
            total += sums[rows * j : rows * (j + 1)]
    return total


def reorder(value, place):
    rows = value.shape[0]
    sums = nt_dot(jnp.concatenate(split(value), axis=0), place)
    return sums[:rows] + sums[rows : 2 * rows] + sums[2 * rows :]


def direction_kernel(frame_total, ordered, *refs):
    ends = 2 * len(CHAINS) // PAIR
    sums = refs[:ends]
    own_ref = refs[ends]
    weights = refs[ends + 1 : -2]
    new_ref, direction_ref = refs[-2:]
    r = own_ref.shape[1]
    n = own_ref.shape[2] // 2
    for c, (first, count, _, _) in enumerate(CHAINS):
        stacked = []
        for i in range(count):
            j = c % PAIR * count + i
            g = (sums[2 * (c // PAIR)][j] + sums[2 * (c // PAIR) + 1][j]) * (1.0 / frame_total)
            stacked.append(jnp.concatenate([g[:, :n], g[:, n:]], axis=0))
        if not ordered:
            moved = reorder(jnp.concatenate(stacked, axis=0), weights[-1][c // PAIR])
            stacked = [moved[2 * r * i : 2 * r * (i + 1)] for i in range(count)]
        for i in range(count):
            f = first + i
            if ordered:
                product = exact_dot(stacked[i], weights[0][f])
            else:
                half = n // 2
                product = exact_dot(stacked[i][:, :half], weights[2 * c][i]) + exact_dot(
                    stacked[i][:, half:], weights[2 * c + 1][i]
                )
            real_part = product[:r, :n] - product[r:, n:]
            imag_part = product[:r, n:] + product[r:, :n]
            own = own_ref[f]
            result = own - jnp.concatenate([real_part, imag_part], axis=1)
            direction_ref[f] = result
            new_ref[f] = own + step_size * result


def direction(sums, own, weights, frame_total, ordered):
    shape = jax.ShapeDtypeStruct(own.shape, jnp.float32)
    bins, r, width = own.shape
    return pl.pallas_call(
        functools.partial(direction_kernel, frame_total, ordered),
        in_specs=in_vmem(len(sums) + 1 + len(weights)),
        out_specs=in_vmem(2),
        out_shape=[shape, shape],
        cost_estimate=pl.CostEstimate(
            flops=24 * bins * width * width * 2 * r, bytes_accessed=2 * bins * width * width, transcendentals=0
        ),
        compiler_params=pltpu.CompilerParams(vmem_limit_bytes=VMEM_LIMIT),
        name="direction",
    )(*sums, own, *weights)


def on_device(signal, demix):
    frame_total = signal.shape[-1] * lax.axis_size("frame")
    index = jnp.stack([lax.axis_index("bin") % 2, lax.axis_index("frame")]).astype(jnp.int32)
    index, demix, signal = lax.optimization_barrier((index, demix, signal))
    weights = [demix]
    for iteration in range(ITERS):
        if iteration == 0:
            y, mine, other, place, own = first_sources(index, demix, signal)
        else:
            y, mine, other = next_sources(index, weights, place, signal)
        mine = mine + over_bins(other, 1)
        mine = mine + over_bins(mine, 2)
        other = over_bins(mine, 1)
        parts = {}
        for c in (0, 2, 1, 3):
            parts[c] = gram(index, y, mine, other, place, c)
            y, parts[c] = lax.optimization_barrier((y, parts[c]))
        parts = [parts[c] for c in range(len(CHAINS))]
        sums = reduce_rows(parts)
        own, result = direction(
            sums, own, weights + [place] * iteration, frame_total, iteration == 0
        )
        if iteration + 1 < ITERS:
            weights = gather_rows(own)
    return own, result


def solution(mesh):
    placed = (P("bin", None, None, "frame"), P("bin", None, None))
    return jax.shard_map(
        on_device,
        mesh=mesh,
        in_specs=placed,
        out_specs=(P("bin", "frame", None), P("bin", "frame", None)),
        check_vma=False,
    )
```

```python
import functools

import jax
import jax.numpy as jnp
from jax import lax
from jax.experimental import pallas as pl
from jax.experimental.pallas import tpu as pltpu
from jax.sharding import PartitionSpec as P

BINS = 32
ITERS = 2

step_size = 0.05
small_eps = 1e-06

X1, X3, Y1, Y3, Z1, Z3 = 1, 3, 16, 48, 4, 12
ORDER_A = ((X1, X3, Y1, Y3, Z1, Z3), (Y1, Y3, X1, X3, Z1, Z3))
ORDER_B = ((X3, X1, Y3, Y1, Z3, Z1), (Y3, Y1, X3, X1, Z3, Z1))
CHAINS = ((0, 2, *ORDER_A), (2, 2, *ORDER_A), (4, 2, *ORDER_B), (6, 2, *ORDER_B))
PAIR = 2
LARGE_STEPS = 2
STEPS = 6
GROUP = 64


def place_matrix(index_ref, chain, rows):
    core, me = index_ref[0], index_ref[1]
    r = rows // GROUP
    p = lax.broadcasted_iota(jnp.int32, (rows, 1), 0)
    owner = jnp.zeros((rows, 1), jnp.int32) + me
    for step in range(STEPS):
        mask = jnp.where(core == 0, chain[2][step], chain[3][step])
        bit = (p // (r << (STEPS - 1 - step))) & 1
        owner = owner ^ (bit * mask)
    source = owner * r + (p & (r - 1))
    column = lax.broadcasted_iota(jnp.int32, (rows, rows), 1)
    return jnp.where(source == column, 1.0, 0.0).astype(jnp.bfloat16)


def move(value, mask0, mask1):
    pairs = []
    for b in range(4):
        mask = (mask0, mask1)[b % 2]
        pairs += [(b * GROUP + f, b * GROUP + (f ^ mask)) for f in range(GROUP)]
    return lax.ppermute(value, ("bin", "frame"), pairs)


def exchange(value, chain, step):
    return move(value, chain[2][step], chain[3][step])


def over_bins(value, mask):
    return lax.ppermute(value, "bin", [(b, b ^ mask) for b in range(4)])


def nt_dot(a, b):
    return lax.dot_general(a, b, (((1,), (1,)), ((), ())), preferred_element_type=jnp.float32)


def nn_dot(a, b):
    return lax.dot_general(a, b, (((1,), (0,)), ((), ())), preferred_element_type=jnp.float32)


def tn_dot(a, b):
    return lax.dot_general(a, b, (((0,), (0,)), ((), ())), preferred_element_type=jnp.float32)


VMEM_LIMIT = 32 * 2**20
FIRST_LIMIT = 45 * 2**20


def in_vmem(count):
    return [pl.BlockSpec(memory_space=pltpu.VMEM)] * count


def add_sources(f, wb, real_x, imag_x, y_ref, power):
    frames = real_x.shape[-1]
    real_y = nn_dot(wb, jnp.concatenate([real_x, -imag_x], axis=0))
    imag_y = nn_dot(wb, jnp.concatenate([imag_x, real_x], axis=0))
    y_ref[f, :, :frames] = real_y
    y_ref[f, :, frames:] = imag_y
    squares = real_y * real_y + imag_y * imag_y
    power[...] = squares if f == 0 else power[...] + squares


def share_power(core_ref, mine_ref, other_ref, power):
    half = power.shape[0] // 2
    core = core_ref[0]
    mine_ref[...] = power[pl.ds(pl.multiple_of(core * half, half), half), :]
    other_ref[...] = power[pl.ds(pl.multiple_of((1 - core) * half, half), half), :]


def first_sources_kernel(core_ref, w_hbm, x_ref, y_ref, mine_ref, other_ref, place_ref, w_ref, power, w_sem):
    bins = w_ref.shape[0]
    copies = [pltpu.make_async_copy(w_hbm.at[f], w_ref.at[f], w_sem.at[f]) for f in range(bins)]
    for copy in copies:
        copy.start()
    for c, chain in enumerate(CHAINS[::PAIR]):
        place_ref[c] = place_matrix(core_ref, chain, w_ref.shape[1])
    for f in range(bins):
        copies[f].wait()
        add_sources(f, w_ref[f].astype(jnp.bfloat16), x_ref[f, 0], x_ref[f, 1], y_ref, power)
    share_power(core_ref, mine_ref, other_ref, power)


def next_sources_kernel(core_ref, *refs):
    pieces = refs[: 2 * len(CHAINS)]
    place_ref, x_ref, y_ref, mine_ref, other_ref, power = refs[2 * len(CHAINS) :]
    for c, chain in enumerate(CHAINS):
        for i in range(chain[1]):
            f = chain[0] + i
            low = pieces[2 * c][i].astype(jnp.bfloat16)
            high = pieces[2 * c + 1][i].astype(jnp.bfloat16)
            wb = tn_dot(place_ref[c // PAIR], jnp.concatenate([low, high], axis=0)).astype(jnp.bfloat16)
            add_sources(f, wb, x_ref[f, 0], x_ref[f, 1], y_ref, power)
    share_power(core_ref, mine_ref, other_ref, power)


def sources_shapes(bins, rows, frames):
    half = jax.ShapeDtypeStruct((rows // 2, frames), jnp.float32)
    return [jax.ShapeDtypeStruct((bins, rows, 2 * frames), jnp.float32), half, half]


def first_sources(core, demix, signal):
    bins, rows, width = demix.shape
    frames = signal.shape[-1]
    return pl.pallas_call(
        first_sources_kernel,
        in_specs=[pl.BlockSpec(memory_space=pltpu.SMEM), pl.BlockSpec(memory_space=pl.ANY)] + in_vmem(1),
        out_specs=in_vmem(4),
        out_shape=sources_shapes(bins, rows, frames)
        + [jax.ShapeDtypeStruct((len(CHAINS) // PAIR, rows, rows), jnp.bfloat16)],
        scratch_shapes=[
            pltpu.VMEM(demix.shape, demix.dtype),
            pltpu.VMEM((rows, frames), jnp.float32),
            pltpu.SemaphoreType.DMA((bins,)),
        ],
        cost_estimate=pl.CostEstimate(
            flops=2 * bins * rows * width * 2 * frames, bytes_accessed=8 * bins * rows * width, transcendentals=0
        ),
        compiler_params=pltpu.CompilerParams(vmem_limit_bytes=FIRST_LIMIT),
        name="first_sources",
    )(core, demix, signal)


def next_sources(core, pieces, place, signal):
    bins, _, rows, frames = signal.shape
    return pl.pallas_call(
        next_sources_kernel,
        in_specs=[pl.BlockSpec(memory_space=pltpu.SMEM)] + in_vmem(len(pieces) + 2),
        out_specs=in_vmem(3),
        out_shape=sources_shapes(bins, rows, frames),
        scratch_shapes=[pltpu.VMEM((rows, frames), jnp.float32)],
        cost_estimate=pl.CostEstimate(
            flops=3 * bins * rows * 2 * rows * 2 * frames, bytes_accessed=8 * bins * rows * 2 * frames, transcendentals=0
        ),
        compiler_params=pltpu.CompilerParams(vmem_limit_bytes=VMEM_LIMIT),
        name="next_sources",
    )(core, *pieces, place, signal)


def gram_kernel(c, core_ref, y_ref, mine_ref, other_ref, place_ref, keep_ref, send_ref, inverse):
    half, frames = mine_ref.shape
    first = CHAINS[c][0]
    core = core_ref[0]
    for ref, at in ((mine_ref, core), (other_ref, 1 - core)):
        radius = jnp.sqrt(ref[...] / BINS + small_eps)
        inverse[pl.ds(pl.multiple_of(at * half, half), half), :] = 1.0 / radius
    for i in range(keep_ref.shape[0]):
        real_y = y_ref[first + i, :, :frames]
        imag_y = y_ref[first + i, :, frames:]
        scale = inverse[...]
        scored = jnp.concatenate(
            [(real_y * scale).astype(jnp.bfloat16), (imag_y * scale).astype(jnp.bfloat16)], axis=1
        )
        scored = nn_dot(place_ref[c // PAIR], scored).astype(jnp.bfloat16)
        real_b = real_y.astype(jnp.bfloat16)
        imag_b = imag_y.astype(jnp.bfloat16)
        real_g = nt_dot(scored, jnp.concatenate([real_b, imag_b], axis=1))
        imag_g = nt_dot(scored, jnp.concatenate([-imag_b, real_b], axis=1))
        rows = 2 * half
        send_ref[i, :, :rows] = real_g[half:]
        send_ref[i, :, rows:] = imag_g[half:]
        keep_ref[i, :, :rows] = real_g[:half]
        keep_ref[i, :, rows:] = imag_g[:half]


def gram(core, y, mine, other, place, c):
    _, rows, both = y.shape
    count = CHAINS[c][1]
    out_shape = jax.ShapeDtypeStruct((count, rows // 2, 2 * rows), jnp.float32)
    return pl.pallas_call(
        functools.partial(gram_kernel, c),
        in_specs=[pl.BlockSpec(memory_space=pltpu.SMEM)] + in_vmem(4),
        out_specs=in_vmem(2),
        out_shape=[out_shape, out_shape],
        scratch_shapes=[pltpu.VMEM((rows, both // 2), jnp.float32)],
        cost_estimate=pl.CostEstimate(
            flops=3 * count * rows * both * 2 * rows, bytes_accessed=count * rows * 4 * both, transcendentals=rows * both
        ),
        compiler_params=pltpu.CompilerParams(vmem_limit_bytes=VMEM_LIMIT),
        name="gram",
    )(core, y, mine, other, place)


def reduce_rows(parts):
    ends = []
    for p in range(0, len(CHAINS), PAIR):
        halves = []
        for (keep, send), chain in zip(parts[p : p + PAIR], CHAINS[p : p + PAIR]):
            for step in range(LARGE_STEPS):
                received = exchange(send, chain, step)
                half = keep.shape[1] // 2
                send = keep[:, half:] + received[:, half:]
                keep = keep[:, :half] + received[:, :half]
            halves.append((keep, send))
        keep, send = (jnp.concatenate(both, axis=0) for both in zip(*halves))
        for step in range(LARGE_STEPS, STEPS):
            received = exchange(send, CHAINS[p], step)
            if step + 1 < STEPS:
                half = keep.shape[1] // 2
                send = keep[:, half:] + received[:, half:]
                keep = keep[:, :half] + received[:, :half]
        ends += [keep, received]
    return ends


def joined(first, second):
    return lax.optimization_barrier(jnp.concatenate([first, second], axis=1))


def gather_rows(own):
    first, second = CHAINS[0][2][4:]
    from_z = {0: own}
    for mask in (first, second, first ^ second):
        from_z[mask] = move(own, mask, mask)
    pieces = []
    for p in range(0, len(CHAINS), PAIR):
        chain = CHAINS[p]
        first, second = chain[2][4:]
        span = slice(chain[0], chain[0] + PAIR * chain[1])
        order = (0, second, first, first ^ second)
        rows = lax.optimization_barrier(jnp.concatenate([from_z[m][span] for m in order], axis=1))
        for step in reversed(range(LARGE_STEPS + 1, STEPS - 2)):
            rows = joined(rows, exchange(rows, chain, step))
        received = exchange(rows, chain, LARGE_STEPS)
        for c in range(PAIR):
            bins = slice(c * chain[1], (c + 1) * chain[1])
            piece = joined(rows[bins], received[bins])
            for step in reversed(range(1, LARGE_STEPS)):
                piece = joined(piece, exchange(piece, chain, step))
            pieces += [piece, exchange(piece, chain, 0)]
    return pieces


def split(value):
    high = value.astype(jnp.bfloat16)
    rest = value - high.astype(jnp.float32)
    middle = rest.astype(jnp.bfloat16)
    low = (rest - middle.astype(jnp.float32)).astype(jnp.bfloat16)
    return high, middle, low


def exact_dot(a, b):
    rows = a.shape[0]
    parts = split(a)
    total = 0.0
    for i, part in enumerate(split(b)):
        sums = nn_dot(jnp.concatenate(parts[: 3 - i], axis=0), part)
        for j in range(3 - i):
            total += sums[rows * j : rows * (j + 1)]
    return total


def reorder(value, place):
    rows = value.shape[0]
    sums = nt_dot(jnp.concatenate(split(value), axis=0), place)
    return sums[:rows] + sums[rows : 2 * rows] + sums[2 * rows :]


def direction_kernel(frame_total, ordered, *refs):
    ends = 2 * len(CHAINS) // PAIR
    sums = refs[:ends]
    own_ref = refs[ends]
    weights = refs[ends + 1 : -2]
    new_ref, direction_ref = refs[-2:]
    r = own_ref.shape[1]
    n = own_ref.shape[2] // 2
    for c, (first, count, _, _) in enumerate(CHAINS):
        stacked = []
        for i in range(count):
            j = c % PAIR * count + i
            g = (sums[2 * (c // PAIR)][j] + sums[2 * (c // PAIR) + 1][j]) * (1.0 / frame_total)
            stacked.append(jnp.concatenate([g[:, :n], g[:, n:]], axis=0))
        if not ordered:
            moved = reorder(jnp.concatenate(stacked, axis=0), weights[-1][c // PAIR])
            stacked = [moved[2 * r * i : 2 * r * (i + 1)] for i in range(count)]
        for i in range(count):
            f = first + i
            if ordered:
                product = exact_dot(stacked[i], weights[0][f])
            else:
                half = n // 2
                product = exact_dot(stacked[i][:, :half], weights[2 * c][i]) + exact_dot(
                    stacked[i][:, half:], weights[2 * c + 1][i]
                )
            real_part = product[:r, :n] - product[r:, n:]
            imag_part = product[:r, n:] + product[r:, :n]
            own = own_ref[f]
            result = own - jnp.concatenate([real_part, imag_part], axis=1)
            direction_ref[f] = result
            new_ref[f] = own + step_size * result


def direction(sums, own, weights, frame_total, ordered):
    shape = jax.ShapeDtypeStruct(own.shape, jnp.float32)
    bins, r, width = own.shape
    return pl.pallas_call(
        functools.partial(direction_kernel, frame_total, ordered),
        in_specs=in_vmem(len(sums) + 1 + len(weights)),
        out_specs=in_vmem(2),
        out_shape=[shape, shape],
        cost_estimate=pl.CostEstimate(
            flops=24 * bins * width * width * 2 * r, bytes_accessed=2 * bins * width * width, transcendentals=0
        ),
        compiler_params=pltpu.CompilerParams(vmem_limit_bytes=VMEM_LIMIT),
        name="direction",
    )(*sums, own, *weights)


def on_device(signal, demix):
    frame_total = signal.shape[-1] * lax.axis_size("frame")
    r = demix.shape[1] // GROUP
    me = lax.axis_index("frame")
    index = jnp.stack([lax.axis_index("bin") % 2, me]).astype(jnp.int32)
    own = lax.dynamic_slice_in_dim(demix, me * r, r, 1)
    index, own, demix, signal = lax.optimization_barrier((index, own, demix, signal))
    weights = [demix]
    for iteration in range(ITERS):
        if iteration == 0:
            y, mine, other, place = first_sources(index, demix, signal)
        else:
            y, mine, other = next_sources(index, weights, place, signal)
        mine = mine + over_bins(other, 1)
        mine = mine + over_bins(mine, 2)
        other = over_bins(mine, 1)
        parts = {}
        for c in (0, 2, 1, 3):
            parts[c] = gram(index, y, mine, other, place, c)
            y, parts[c] = lax.optimization_barrier((y, parts[c]))
        parts = [parts[c] for c in range(len(CHAINS))]
        sums = reduce_rows(parts)
        own, result = direction(
            sums, own, weights + [place] * iteration, frame_total, iteration == 0
        )
        if iteration + 1 < ITERS:
            weights = gather_rows(own)
    return own, result


def solution(mesh):
    placed = (P("bin", None, None, "frame"), P("bin", None, None))
    return jax.shard_map(
        on_device,
        mesh=mesh,
        in_specs=placed,
        out_specs=(P("bin", "frame", None), P("bin", "frame", None)),
        check_vma=False,
    )
```
